256 devices in a mesh: occ: 32 (over y_lo, z, core), aux: 4 (over x), vir: 2 (over y_hi).
Axes of the slice: x: 4, y: 4 (y_hi: 2, y_lo: 2; y = y_hi * 2 + y_lo), z: 8, core: 2. Of those that a mesh axis runs over, the one named last changes fastest.
Arguments:
- integrals: bfloat16 [32, 2048, 4096], P('occ', 'vir', 'aux'), may hold values from -0.65625 to 0.65625
- occ_energy: float32 [32], replicated, may hold values from -2 to -0.5
- vir_energy: float32 [2048], replicated, may hold values from 0.25 to 3
Outputs:
- lagrangian: bfloat16 [32, 2048, 4096], P('occ', 'vir', 'aux')
The draws below stay inside these ranges and needn't reach their ends.
All inputs are finite; a program needn't handle non-finite values.
Results may differ from the reference program's by a relative error of at most 0.0039.
Values may be sent and summed in bfloat16 or wider, within the bound.
A program may use at most 64 MiB of HBM per device.

```python
import jax
import jax.numpy as jnp
from jax import lax

V = 2048
NAUX = 4096
OCC_DEV = 1
NOCC = 32


def shard_levels(own_key, shape, cuts, least, high):
    def one(axis_at, blocks):
        steps = jax.random.uniform(jax.random.fold_in(jax.random.fold_in(own_key, 6), axis_at), (blocks,), jnp.float32, least / len(cuts), high / len(cuts))
        return jnp.repeat(jnp.exp(steps), shape[axis_at] // blocks).reshape((-1,) + (1,) * (len(shape) - axis_at - 1))

    factor_of = one(*cuts[0])
    for cut in cuts[1:]:
        factor_of = factor_of * one(*cut)
    return factor_of


def noise(rng, shape, scale, most, pieces=(), kind=jnp.bfloat16):
    array = scale * jax.random.normal(rng, shape, jnp.float32)
    if pieces:
        array = array * shard_levels(rng, shape, pieces, -0.22, 0.18)
    return jnp.clip(array, -most, most).astype(kind)


def setup_inputs(seed: int = 0) -> dict:
    seeds = jax.random.split(jax.random.key(seed), 4)
    return {
        "integrals": noise(seeds[0], (NOCC, V, NAUX), 0.11, 0.65625, ((0, 32), (1, 2), (2, 4))),
        "occ_energy": jnp.clip(jax.random.uniform(seeds[1], (NOCC,), jnp.float32, -2.0, -0.5), -2.0, -0.5),
        "vir_energy": jnp.clip(jax.random.uniform(seeds[2], (V,), jnp.float32, 0.25, 3.0), 0.25, 3.0),
    }


def pair_block(own_rows, partner_rows, own_level, partner_level, vir_energy):
    pair_values = jnp.dot(own_rows, partner_rows.T, preferred_element_type=jnp.float32)
    denominator = own_level + partner_level - vir_energy[:, None] - vir_energy[None, :]
    amplitudes = (pair_values / denominator).astype(jnp.bfloat16)
    own_part = jnp.dot(amplitudes, partner_rows, preferred_element_type=jnp.float32)
    back_part = jnp.dot(amplitudes.T, own_rows, preferred_element_type=jnp.float32)
    return own_part, back_part


def reference(integrals, occ_energy, vir_energy):
    distance = 2 * OCC_DEV
    partner = jnp.roll(integrals, distance, axis=0)
    partner_energy = jnp.roll(occ_energy, distance)

    def one_pair(inputs):
        return pair_block(inputs[0], inputs[1], inputs[2], inputs[3], vir_energy)

    own_part, back_part = lax.map(one_pair, (integrals, partner, occ_energy, partner_energy))
    back_rows = jnp.roll(back_part, -distance, axis=0)
    return (own_part + back_rows).astype(jnp.bfloat16)
```

```python
import functools

import jax
import jax.numpy as jnp
from jax import lax
from jax.experimental import pallas as pl
from jax.experimental.pallas import tpu as pltpu
from jax.sharding import PartitionSpec as P

MESH = pl.DeviceIdType.MESH
BF16 = jnp.bfloat16
F32 = jnp.float32

K = 4
R = 256
W = 2 * R
S = R // 4
H = S // 2
SLOTS = 4

TILES = [(0, 0)]
for k in range(1, K):
    for j in range(k):
        TILES += [(k, j), (j, k)]
    TILES += [(k, k)]
NT = len(TILES)
ROW_END = {a: max(t for t, tile in enumerate(TILES) if tile[0] == a) for a in range(K)}
COL_END = {b: max(t for t, tile in enumerate(TILES) if tile[1] == b) for b in range(K)}

OFF = {"A": 0, "B": 1, "C": 2, "D": 3, "E": 4}


def kernel(
    x_ref, acol_ref, brow_ref, out_ref,
    bi, bp, vf, s1, s2, r1, r2, tt, own, back, cr, zs, zr, os_,
    in_s, in_r, zi_s, zi_r, ci_s, ci_r, x_s, x_r, cb_s, cb_r, zb_s, zb_r, o_s, o_r,
):
    o, x, v = lax.axis_index("occ"), lax.axis_index("aux"), lax.axis_index("vir")
    c = lax.rem(o, 2)
    cross = c + v == 1
    straight = c + v != 1
    flip = o + 1 - 2 * c
    xp = (o, lax.rem(x + 1, 4), v)
    xm = (o, lax.rem(x + 3, 4), v)
    zp = (lax.rem(o + 2, 32), x, v)
    zm = (lax.rem(o + 30, 32), x, v)
    core = (flip, x, v)
    swap = (flip, x, 1 - v)

    def remote(src, dst, ssem, rsem, to):
        return pltpu.make_async_remote_copy(
            src_ref=src, dst_ref=dst, send_sem=ssem, recv_sem=rsem, device_id=to, device_id_type=MESH
        )

    barrier = pltpu.get_barrier_semaphore()
    for peer in (xp, xm, zp, zm, core, swap):
        pl.semaphore_signal(barrier, inc=1, device_id=peer, device_id_type=MESH)
    pl.semaphore_wait(barrier, 6)

    def rows(k):
        return pl.ds(k * R, R)

    def in_remote(k):
        return remote(x_ref.at[rows(k)], bi.at[k], in_s.at[k], in_r.at[k], swap)

    def in_local(k):
        return pltpu.make_async_copy(x_ref.at[rows(k)], bi.at[k], in_r.at[k])

    def out_remote(k):
        return remote(os_.at[k], out_ref.at[rows(k)], o_s.at[k], o_r.at[k], swap)

    def out_local(k):
        return pltpu.make_async_copy(os_.at[k], out_ref.at[rows(k)], o_r.at[k])

    def z_in(k):
        return remote(bi.at[k], bp.at[0, k], zi_s.at[k], zi_r.at[k], zp)

    def c_in(k):
        return remote(bp.at[0, k], bp.at[1, k], ci_s.at[k], ci_r.at[k], core)

    def c_back(k):
        return remote(back.at[1, k], cr.at[k], cb_s.at[k], cb_r.at[k], core)

    def z_back(k):
        return remote(zs.at[k], zr.at[k], zb_s.at[k], zb_r.at[k], zm)

    far = lax.rem(x + 2, 4)
    low = lax.rem(x + 3, 4)
    high = lax.rem(x + 1, 4)

    def part(shard, first, count):
        return pl.ds(pl.multiple_of(shard * S + first, H), count)

    def rs1(t):
        return (
            remote(s1.at[t, pl.ds(0, H)], r1.at[t, 0], x_s.at[0, t], x_r.at[0, t], xm),
            remote(s1.at[t, pl.ds(H, H)], r1.at[t, 1], x_s.at[1, t], x_r.at[1, t], xp),
        )

    def rs2(t):
        return (
            remote(s2.at[t, 0], r2.at[t, 0], x_s.at[2, t], x_r.at[2, t], xm),
            remote(s2.at[t, 1], r2.at[t, 1], x_s.at[3, t], x_r.at[3, t], xp),
        )

    def ag1(t):
        mine = tt.at[t, part(x, 0, S)]
        return (
            remote(mine, mine, x_s.at[4, t], x_r.at[4, t], xm),
            remote(mine, mine, x_s.at[5, t], x_r.at[5, t], xp),
        )

    def ag2(t):
        up = tt.at[t, part(low, 0, H)]
        down = tt.at[t, part(high, H, H)]
        return (
            remote(down, down, x_s.at[6, t], x_r.at[6, t], xm),
            remote(up, up, x_s.at[7, t], x_r.at[7, t], xp),
        )

    def start(copies):
        for copy in copies:
            copy.start()

    def wait_recv(copies):
        for copy in copies:
            copy.wait_recv()

    @pl.when(cross)
    def _():
        for k in range(K):
            in_remote(k).start()

    @pl.when(straight)
    def _():
        for k in range(K):
            in_local(k).start()

    def forward(k):
        @pl.when(cross)
        def _():
            in_remote(k).wait_recv()

        @pl.when(straight)
        def _():
            in_local(k).wait()

        z_in(k).start()

    def spread(k):
        z_in(k).wait_recv()
        c_in(k).start()

    def nt(a, b):
        return lax.dot_general(a, b, (((1,), (1,)), ((), ())), preferred_element_type=F32)

    def tn(a, b):
        return lax.dot_general(a, b, (((0,), (0,)), ((), ())), preferred_element_type=F32)

    def nn(a, b):
        return lax.dot_general(a, b, (((1,), (0,)), ((), ())), preferred_element_type=F32)

    def stage_a(t):
        a, b = TILES[t]
        slot = t % SLOTS
        for half in (0, 1):
            vf[slot, :, half * R : (half + 1) * R] = nt(bi[a], bp[half, b])
        s1[t] = vf[slot, part(far, 0, S), :].astype(BF16)
        start(rs1(t))

    def stage_b(t):
        slot = t % SLOTS
        wait_recv(rs1(t))
        s2[t, 0, 0:H] = (vf[slot, part(low, 0, H), :] + r1[t, 0].astype(F32)).astype(BF16)
        s2[t, 0, H:S] = vf[slot, part(low, H, H), :].astype(BF16)
        s2[t, 1, 0:H] = vf[slot, part(high, 0, H), :].astype(BF16)
        s2[t, 1, H:S] = (vf[slot, part(high, H, H), :] + r1[t, 1].astype(F32)).astype(BF16)
        start(rs2(t))

    def stage_c(t):
        a, b = TILES[t]
        slot = t % SLOTS
        wait_recv(rs2(t))
        total = vf[slot, part(x, 0, S), :] + r2[t, 0].astype(F32) + r2[t, 1].astype(F32)
        level = acol_ref[pl.ds(pl.multiple_of(a * R + x * S, S), S), :]
        for half in (0, 1):
            cols = slice(half * R, (half + 1) * R)
            gap = level - brow_ref[half : half + 1, b * R : (b + 1) * R]
            tt[t, part(x, 0, S), cols] = (total[:, cols] / gap).astype(BF16)
        start(ag1(t))

    def stage_d(t):
        wait_recv(ag1(t))
        start(ag2(t))

    def stage_e(t):
        a, b = TILES[t]
        wait_recv(ag2(t))
        first_row = all(tile[0] != a for tile in TILES[:t])
        first_col = all(tile[1] != b for tile in TILES[:t])
        for half in (0, 1):
            term = tn(tt[t, :, half * R : (half + 1) * R], bi[a])
            if first_col:
                back[half, b] = term
            else:
                back[half, b] += term
        if COL_END[b] == t:
            c_back(b).start()
        term = nn(tt[t, :, 0:R], bp[0, b]) + nn(tt[t, :, R:W], bp[1, b])
        if first_row:
            own[a] = term
        else:
            own[a] += term

    def stage_f(k):
        c_back(k).wait_recv()
        zs[k] = (back[0, k] + cr[k]).astype(BF16)
        z_back(k).start()

    def stage_g(k):
        z_back(k).wait_recv()
        os_[k] = (own[k] + zr[k].astype(F32)).astype(BF16)

        @pl.when(cross)
        def _():
            out_remote(k).start()

        @pl.when(straight)
        def _():
            out_local(k).start()

    arrived = set()
    sent = 0
    last = NT + OFF["E"] + 6
    done_f, done_g = set(), set()
    for it in range(last):
        for k in range(K):
            if k not in done_f and it - OFF["E"] > COL_END[k]:
                stage_f(k)
                done_f.add(k)
        for k in range(K):
            if k not in done_g and k in done_f and it - OFF["E"] > max(COL_END[k] + 2, ROW_END[k]):
                stage_g(k)
                done_g.add(k)
        for name, stage in (("E", stage_e), ("D", stage_d), ("C", stage_c), ("B", stage_b)):
            t = it - OFF[name]
            if 0 <= t < NT:
                stage(t)
        if it < NT:
            a, b = TILES[it]
            while sent <= min(K - 1, max(a, b) + 1):
                if sent > 0 and sent - 1 not in arrived:
                    spread(sent - 1)
                    arrived.add(sent - 1)
                    pending = sent - 1
                else:
                    pending = None
                forward(sent)
                if pending is not None:
                    c_in(pending).wait_recv()
                sent += 1
            for k in (a, b):
                if k not in arrived:
                    spread(k)
                    c_in(k).wait_recv()
                    arrived.add(k)
            stage_a(it)

    for t in range(NT):
        for group in (rs1(t), rs2(t), ag1(t), ag2(t)):
            for copy in group:
                copy.wait_send()
    for k in range(K):
        z_in(k).wait_send()
        c_in(k).wait_send()
        c_back(k).wait_send()
        z_back(k).wait_send()

    @pl.when(cross)
    def _():
        for k in range(K):
            in_remote(k).wait_send()
            out_remote(k).wait()

    @pl.when(straight)
    def _():
        for k in range(K):
            out_local(k).wait()


def on_device(integrals, occ_energy, vir_energy):
    o, v = lax.axis_index("occ"), lax.axis_index("vir")
    core = lax.rem(o, 2)
    i = o - core + v
    level = lax.dynamic_slice_in_dim(occ_energy, i, 1) + lax.dynamic_slice_in_dim(
        occ_energy, lax.rem(i + 30, 32), 1
    )
    halves = vir_energy.reshape(2, 1024)
    mine = lax.dynamic_slice_in_dim(vir_energy, core * 1024, 1024)
    other = lax.dynamic_slice_in_dim(vir_energy, (1 - core) * 1024, 1024)
    acol = (level - mine)[:, None]
    brow = jnp.stack([mine, other])
    dma = pltpu.SemaphoreType.DMA
    vmem = pltpu.VMEM
    out = pl.pallas_call(
        kernel,
        out_shape=jax.ShapeDtypeStruct((1024, 1024), BF16),
        in_specs=[
            pl.BlockSpec(memory_space=pl.ANY),
            pl.BlockSpec(memory_space=pltpu.VMEM),
            pl.BlockSpec(memory_space=pltpu.VMEM),
        ],
        out_specs=pl.BlockSpec(memory_space=pl.ANY),
        scratch_shapes=[
            vmem((K, R, 1024), BF16),
            vmem((2, K, R, 1024), BF16),
            vmem((SLOTS, R, W), F32),
            vmem((NT, S, W), BF16),
            vmem((NT, 2, S, W), BF16),
            vmem((NT, 2, H, W), BF16),
            vmem((NT, 2, S, W), BF16),
            vmem((NT, R, W), BF16),
            vmem((K, R, 1024), F32),
            vmem((2, K, R, 1024), F32),
            vmem((K, R, 1024), F32),
            vmem((K, R, 1024), BF16),
            vmem((K, R, 1024), BF16),
            vmem((K, R, 1024), BF16),
            dma((K,)), dma((K,)), dma((K,)), dma((K,)), dma((K,)), dma((K,)),
            dma((8, NT)), dma((8, NT)),
            dma((K,)), dma((K,)), dma((K,)), dma((K,)), dma((K,)), dma((K,)),
        ],
        compiler_params=pltpu.CompilerParams(
            collective_id=0, has_side_effects=True, vmem_limit_bytes=58 * 2**20
        ),
        cost_estimate=pl.CostEstimate(flops=13 * 10**9, bytes_accessed=4 * 2**20, transcendentals=0),
        name="pair_lagrangian",
    )(integrals.reshape(1024, 1024), acol, brow)
    return out.reshape(1, 1024, 1024)


def solution(mesh):
    placed = (P("occ", "vir", "aux"), P(), P())
    return jax.shard_map(
        on_device, mesh=mesh, in_specs=placed, out_specs=P("occ", "vir", "aux"), check_vma=False
    )
```

```python
import functools

import jax
import jax.numpy as jnp
from jax import lax
from jax.experimental import pallas as pl
from jax.experimental.pallas import tpu as pltpu
from jax.sharding import PartitionSpec as P

MESH = pl.DeviceIdType.MESH
BF16 = jnp.bfloat16
F32 = jnp.float32

N = 1024
R = 256
S = R // 4
H = S // 2
SLOTS = 6

SIZES = [128, 128, 256, 256, 128, 128]
K = len(SIZES)
START = [sum(SIZES[:k]) for k in range(K)]
ROWS = N // R
NEEDS = [[k for k in range(K) if START[k] // R == a] for a in range(ROWS)]

TILES = [(0, 0), (1, 0), (0, 1), (1, 1), (2, 0), (2, 1), (3, 0), (3, 1)]
TILES += [(a, b) for b in range(2, K) for a in range(ROWS)]
NT = len(TILES)
WIDE = max(SIZES)
KIND = [0 if SIZES[b] == WIDE else 1 for a, b in TILES]
PLACE = [KIND[:t].count(KIND[t]) for t in range(NT)]
COUNT = [KIND.count(0), KIND.count(1)]
ROW_END = [max(t for t, tile in enumerate(TILES) if tile[0] == a) for a in range(ROWS)]
COL_END = [max(t for t, tile in enumerate(TILES) if tile[1] == b) for b in range(K)]

OFF = {"A": 0, "B": 2, "C": 4, "D": 6, "E": 7}
FORWARD = {0: [0, 1], 1: [2], 2: [3], 4: [4], 5: [5]}
DIRECT = {0: [0, 1], 4: [2], 6: [3], 8: [4], 10: [5]}
SPREAD = {0: [0], 2: [1], 5: [2], 9: [3], 12: [4], 14: [5]}


def kernel(
    x_ref, occ_ref, vir_ref, out_ref,
    bi, bp, acol, vf, s1w, s1n, s2w, s2n, r1w, r1n, r2w, r2n, ttw, ttn, own, back, cr, zs, zr, os_, ow, os2,
    in_s, in_r, zi_s, zi_r, ci_s, ci_r, x_s, x_r, cb_s, cb_r, zb_s, zb_r, o_s, o_r, w_s, w_r,
):
    o, x, v = lax.axis_index("occ"), lax.axis_index("aux"), lax.axis_index("vir")
    c = lax.rem(o, 2)
    base = o - c
    z = lax.rem(o, 16) // 2
    last = z // 7
    first = 1 - (z + 7) // 8
    cross = c + v == 1
    straight = c + v != 1
    cross_last = lax.rem(c + v, 2) + last == 2
    cross_inner = lax.rem(c + v, 2) - last == 1
    xp = (o, lax.rem(x + 1, 4), v)
    xm = (o, lax.rem(x + 3, 4), v)
    zp = (lax.rem(base + 2, 32) + c + last * (v - c), x, v + last * (c - v))
    zm = (lax.rem(base + 30, 32) + c + first * (v - c), x, v + first * (c - v))
    core = (base + 1 - c, x, v)
    swap = (base + 1 - c, x, 1 - v)
    s1, s2, r1, r2, tt = (s1w, s1n), (s2w, s2n), (r1w, r1n), (r2w, r2n), (ttw, ttn)

    def remote(src, dst, ssem, rsem, to):
        return pltpu.make_async_remote_copy(
            src_ref=src, dst_ref=dst, send_sem=ssem, recv_sem=rsem, device_id=to, device_id_type=MESH
        )

    barrier = pltpu.get_barrier_semaphore()
    for peer in (xp, xm, zp, zm, core, swap):
        pl.semaphore_signal(barrier, inc=1, device_id=peer, device_id_type=MESH)
    pl.semaphore_wait(barrier, 6)

    def rows(k):
        return pl.ds(START[k], SIZES[k])

    def pair(k, half):
        return pl.ds(2 * START[k] + half * SIZES[k], SIZES[k])

    def in_remote(k):
        return remote(x_ref.at[rows(k)], bi.at[rows(k)], in_s.at[k], in_r.at[k], swap)

    def in_local(k):
        return pltpu.make_async_copy(x_ref.at[rows(k)], bi.at[rows(k)], in_r.at[k])

    def z_in(k):
        return remote(bi.at[rows(k)], bp.at[pair(k, 0)], zi_s.at[k], zi_r.at[k], zp)

    def z_direct(k):
        return remote(x_ref.at[rows(k)], bp.at[pair(k, 0)], zi_s.at[k], zi_r.at[k], zp)

    def c_in(k):
        return remote(bp.at[pair(k, 0)], bp.at[pair(k, 1)], ci_s.at[k], ci_r.at[k], core)

    def c_back(k):
        return remote(back.at[pair(k, 1)], cr.at[rows(k)], cb_s.at[k], cb_r.at[k], core)

    def z_back(k):
        return remote(zs.at[rows(k)], zr.at[rows(k)], zb_s.at[k], zb_r.at[k], zm)

    def out_remote(k):
        return remote(os_.at[rows(k)], out_ref.at[rows(k)], o_s.at[k], o_r.at[k], swap)

    def out_local(k):
        return pltpu.make_async_copy(os_.at[rows(k)], out_ref.at[rows(k)], o_r.at[k])

    def own_remote(k):
        return remote(os_.at[rows(k)], ow.at[rows(k)], w_s.at[k], w_r.at[k], swap)

    def out_sum(k):
        return pltpu.make_async_copy(os2.at[rows(k)], out_ref.at[rows(k)], o_r.at[k])

    far = lax.rem(x + 2, 4)
    low = lax.rem(x + 3, 4)
    high = lax.rem(x + 1, 4)

    def part(shard, begin, count):
        return pl.ds(pl.multiple_of(shard * S + begin, H), count)

    def of(refs, t):
        return refs[KIND[t]].at[PLACE[t]]

    def rs1(t):
        src, dst = of(s1, t), of(r1, t)
        return (
            remote(src.at[pl.ds(0, H)], dst.at[0], x_s.at[0, t], x_r.at[0, t], xm),
            remote(src.at[pl.ds(H, H)], dst.at[1], x_s.at[1, t], x_r.at[1, t], xp),
        )

    def rs2(t):
        src, dst = of(s2, t), of(r2, t)
        return (
            remote(src.at[0], dst.at[0], x_s.at[2, t], x_r.at[2, t], xm),
            remote(src.at[1], dst.at[1], x_s.at[3, t], x_r.at[3, t], xp),
        )

    def ag1(t):
        mine = of(tt, t).at[part(x, 0, S)]
        return (
            remote(mine, mine, x_s.at[4, t], x_r.at[4, t], xm),
            remote(mine, mine, x_s.at[5, t], x_r.at[5, t], xp),
        )

    def ag2(t):
        up = of(tt, t).at[part(low, 0, H)]
        down = of(tt, t).at[part(high, H, H)]
        return (
            remote(down, down, x_s.at[6, t], x_r.at[6, t], xm),
            remote(up, up, x_s.at[7, t], x_r.at[7, t], xp),
        )

    def start(copies):
        for copy in copies:
            copy.start()

    def wait_recv(copies):
        for copy in copies:
            copy.wait_recv()

    for k in range(K):
        @pl.when(cross)
        def _():
            in_remote(k).start()

        @pl.when(straight)
        def _():
            in_local(k).start()

    def direct(k):
        @pl.when(last == 1)
        def _():
            z_direct(k).start()

    def forward(k):
        @pl.when(cross)
        def _():
            in_remote(k).wait_recv()

        @pl.when(straight)
        def _():
            in_local(k).wait()

        @pl.when(last == 0)
        def _():
            z_in(k).start()

    def spread(k):
        z_in(k).wait_recv()
        c_in(k).start()

    def dot(a, b, over):
        return lax.dot_general(a, b, ((over[:1], over[1:]), ((), ())), preferred_element_type=F32)

    level = occ_ref[base + v] + occ_ref[lax.rem(base + v + 30, 32)]
    for j in range(N // 128):
        lanes = pl.ds(pl.multiple_of(c * N + j * 128, 128), 128)
        acol[j * 128 : (j + 1) * 128, :] = jnp.broadcast_to(level - vir_ref[0:1, lanes], (128, 128)).T

    def stage_a(t):
        a, b = TILES[t]
        width = 2 * SIZES[b]
        slot = t % SLOTS
        vf[slot, :, 0:width] = dot(
            bi[a * R : (a + 1) * R], bp[2 * START[b] : 2 * START[b] + width], (1, 1)
        )
        of(s1, t)[...] = vf[slot, part(far, 0, S), 0:width].astype(BF16)
        start(rs1(t))

    def stage_b(t):
        slot = t % SLOTS
        width = 2 * SIZES[TILES[t][1]]
        wait_recv(rs1(t))
        got, put = of(r1, t), of(s2, t)
        put[0, 0:H] = (vf[slot, part(low, 0, H), 0:width] + got[0].astype(F32)).astype(BF16)
        put[0, H:S] = vf[slot, part(low, H, H), 0:width].astype(BF16)
        put[1, 0:H] = vf[slot, part(high, 0, H), 0:width].astype(BF16)
        put[1, H:S] = (vf[slot, part(high, H, H), 0:width] + got[1].astype(F32)).astype(BF16)
        start(rs2(t))

    def stage_c(t):
        a, b = TILES[t]
        size = SIZES[b]
        slot = t % SLOTS
        wait_recv(rs2(t))
        got, put = of(r2, t), of(tt, t)
        level_a = acol[pl.ds(pl.multiple_of(a * R + x * S, S), S), 0:1]
        for half in (0, 1):
            cols = slice(half * size, (half + 1) * size)
            total = vf[slot, part(x, 0, S), cols] + got[0, :, cols].astype(F32) + got[1, :, cols].astype(F32)
            begin = (c + half - 2 * c * half) * N + START[b]
            gap = level_a - vir_ref[0:1, pl.ds(pl.multiple_of(begin, 128), size)]
            put[part(x, 0, S), cols] = (total / gap).astype(BF16)
        start(ag1(t))

    def stage_d(t):
        wait_recv(ag1(t))
        start(ag2(t))

    def stage_e(t):
        a, b = TILES[t]
        wait_recv(ag2(t))
        own_rows = slice(a * R, (a + 1) * R)
        pair_rows = slice(2 * START[b], 2 * START[b] + 2 * SIZES[b])
        tile = of(tt, t)[...]
        term = dot(tile, bi[own_rows], (0, 0))
        if all(other[1] != b for other in TILES[:t]):
            back[pair_rows] = term
        else:
            back[pair_rows] += term
        if COL_END[b] == t:
            c_back(b).start()
        term = dot(tile, bp[pair_rows], (1, 0))
        if all(other[0] != a for other in TILES[:t]):
            own[own_rows] = term
        else:
            own[own_rows] += term

    def stage_f(k):
        r = slice(START[k], START[k] + SIZES[k])
        c_back(k).wait_recv()
        zs[r] = (back[2 * START[k] : 2 * START[k] + SIZES[k]] + cr[r]).astype(BF16)
        z_back(k).start()

    def stage_g(k):
        r = slice(START[k], START[k] + SIZES[k])

        @pl.when(cross_last)
        def _():
            os_[r] = own[r].astype(BF16)
            own_remote(k).start()

        @pl.when(lax.rem(c + v, 2) + last != 2)
        def _():
            z_back(k).wait_recv()
            os_[r] = (own[r] + zr[r].astype(F32)).astype(BF16)

            @pl.when(cross)
            def _():
                out_remote(k).start()

            @pl.when(straight)
            def _():
                out_local(k).start()

    def stage_h(k):
        r = slice(START[k], START[k] + SIZES[k])

        @pl.when(cross_last)
        def _():
            own_remote(k).wait_recv()
            z_back(k).wait_recv()
            os2[r] = (ow[r].astype(F32) + zr[r].astype(F32)).astype(BF16)
            out_sum(k).start()

    done_f, done_g = set(), set()
    for it in range(NT + OFF["E"] + 1):
        for name, stage in (("D", stage_d), ("C", stage_c), ("B", stage_b)):
            t = it - OFF[name]
            if 0 <= t < NT:
                stage(t)
        if it < NT:
            a, b = TILES[it]
            for k in DIRECT.get(it, []):
                direct(k)
            for k in FORWARD.get(it, []):
                forward(k)
            for k in SPREAD.get(it, []):
                spread(k)
            if all(other[1] != b for other in TILES[:it]):
                c_in(b).wait_recv()
            stage_a(it)
        t = it - OFF["E"]
        for k in range(K):
            if k not in done_f and t > COL_END[k]:
                stage_f(k)
                done_f.add(k)
        if 0 <= t < NT:
            stage_e(t)
        for k in range(K):
            if k not in done_g and COL_END[k] + 3 <= t and ROW_END[START[k] // R] <= t:
                stage_g(k)
                done_g.add(k)
    for k in range(K):
        if k not in done_f:
            stage_f(k)
    for k in range(K):
        if k not in done_g:
            stage_g(k)
    for k in range(K):
        stage_h(k)

    for t in range(NT):
        for group in (rs1(t), rs2(t), ag1(t), ag2(t)):
            for copy in group:
                copy.wait_send()
    for k in range(K):
        @pl.when(last == 0)
        def _():
            z_in(k).wait_send()

        @pl.when(last == 1)
        def _():
            z_direct(k).wait_send()

        c_in(k).wait_send()
        c_back(k).wait_send()
        z_back(k).wait_send()

        @pl.when(cross)
        def _():
            in_remote(k).wait_send()

        @pl.when(cross_inner)
        def _():
            out_remote(k).wait()

        @pl.when(cross_last)
        def _():
            own_remote(k).wait_send()
            out_sum(k).wait()

        @pl.when(straight)
        def _():
            out_local(k).wait()


def on_device(integrals, occ_energy, vir_energy):
    dma = pltpu.SemaphoreType.DMA
    vmem = pltpu.VMEM

    def tiles(*lead):
        return [vmem((COUNT[kind], *lead, 2 * (WIDE >> kind)), BF16) for kind in (0, 1)]

    out = pl.pallas_call(
        kernel,
        out_shape=jax.ShapeDtypeStruct((N, N), BF16),
        in_specs=[
            pl.BlockSpec(memory_space=pl.ANY),
            pl.BlockSpec(memory_space=pltpu.SMEM),
            pl.BlockSpec(memory_space=pltpu.VMEM),
        ],
        out_specs=pl.BlockSpec(memory_space=pl.ANY),
        scratch_shapes=[
            vmem((N, N), BF16),
            vmem((2 * N, N), BF16),
            vmem((N, 128), F32),
            vmem((SLOTS, R, 2 * WIDE), F32),
            *tiles(S),
            *tiles(2, S),
            *tiles(2, H),
            *tiles(2, S),
            *tiles(R),
            vmem((N, N), F32),
            vmem((2 * N, N), F32),
            vmem((N, N), F32),
            vmem((N, N), BF16),
            vmem((N, N), BF16),
            vmem((N, N), BF16),
            vmem((N, N), BF16),
            vmem((N, N), BF16),
            *[dma((K,))] * 6,
            dma((8, NT)), dma((8, NT)),
            *[dma((K,))] * 8,
        ],
        compiler_params=pltpu.CompilerParams(
            collective_id=0, has_side_effects=True, vmem_limit_bytes=58 * 2**20
        ),
        cost_estimate=pl.CostEstimate(flops=13 * 10**9, bytes_accessed=4 * 2**20, transcendentals=0),
        name="pair_lagrangian",
    )(integrals.reshape(N, N), occ_energy, vir_energy.reshape(1, 2 * N))
    return out.reshape(1, N, N)


def solution(mesh):
    placed = (P("occ", "vir", "aux"), P(), P())
    return jax.shard_map(
        on_device, mesh=mesh, in_specs=placed, out_specs=P("occ", "vir", "aux"), check_vma=False
    )
```

```python
import functools

import jax
import jax.numpy as jnp
from jax import lax
from jax.experimental import pallas as pl
from jax.experimental.pallas import tpu as pltpu
from jax.sharding import PartitionSpec as P

MESH = pl.DeviceIdType.MESH
BF16 = jnp.bfloat16
F32 = jnp.float32

N = 1024
R = 256
S = R // 4
H = S // 2
SLOTS = 6

SIZES = [128, 128, 256, 256, 128, 128]
K = len(SIZES)
START = [sum(SIZES[:k]) for k in range(K)]
ROWS = N // R
NEEDS = [[k for k in range(K) if START[k] // R == a] for a in range(ROWS)]

TILES = [(0, 0), (1, 0), (0, 1), (1, 1), (2, 0), (2, 1), (0, 2), (1, 2), (3, 0), (3, 1), (2, 2), (3, 2)]
TILES += [(a, 3) for a in range(ROWS)] + [(0, 4), (0, 5), (1, 4), (1, 5), (2, 4), (3, 4), (2, 5), (3, 5)]
NT = len(TILES)
WIDE = max(SIZES)
KIND = [0 if SIZES[b] == WIDE else 1 for a, b in TILES]
PLACE = [KIND[:t].count(KIND[t]) for t in range(NT)]
COUNT = [KIND.count(0), KIND.count(1)]
ROW_END = [max(t for t, tile in enumerate(TILES) if tile[0] == a) for a in range(ROWS)]
COL_END = [max(t for t, tile in enumerate(TILES) if tile[1] == b) for b in range(K)]

OFF = {"A": 0, "B": 2, "C": 4, "D": 6, "E": 7}
FORWARD = {0: [0, 1], 1: [2], 3: [3], 5: [4], 6: [5]}
DIRECT = {3: [2], 6: [3], 8: [4], 10: [5]}
SPREAD = {0: [0], 2: [1], 5: [2], 9: [3], 12: [4], 14: [5]}


def kernel(
    x_ref, occ_ref, vir_ref, out_ref,
    bi, bp, acol, vf, s1w, s1n, s2w, s2n, r1w, r1n, r2w, r2n, ttw, ttn, own, back, cr, zs, zr, os_, ow, os2,
    in_s, in_r, zi_s, zi_r, ci_s, ci_r, x_s, x_r, cb_s, cb_r, zb_s, zb_r, o_s, o_r, w_s, w_r,
):
    o, x, v = lax.axis_index("occ"), lax.axis_index("aux"), lax.axis_index("vir")
    c = lax.rem(o, 2)
    base = o - c
    z = lax.rem(o, 16) // 2
    last = z // 7
    first = 1 - (z + 7) // 8
    cross = c + v == 1
    straight = c + v != 1
    straight_last = last - lax.rem(c + v, 2) == 1
    cross_last = lax.rem(c + v, 2) + last == 2
    cross_inner = lax.rem(c + v, 2) - last == 1
    xp = (o, lax.rem(x + 1, 4), v)
    xm = (o, lax.rem(x + 3, 4), v)
    zp = (lax.rem(base + 2, 32) + c + last * (v - c), x, v + last * (c - v))
    zm = (lax.rem(base + 30, 32) + c + first * (v - c), x, v + first * (c - v))
    core = (base + 1 - c, x, v)
    swap = (base + 1 - c, x, 1 - v)
    s1, s2, r1, r2, tt = (s1w, s1n), (s2w, s2n), (r1w, r1n), (r2w, r2n), (ttw, ttn)

    def remote(src, dst, ssem, rsem, to):
        return pltpu.make_async_remote_copy(
            src_ref=src, dst_ref=dst, send_sem=ssem, recv_sem=rsem, device_id=to, device_id_type=MESH
        )

    barrier = pltpu.get_barrier_semaphore()
    for peer in (xp, xm, zp, zm, core, swap):
        pl.semaphore_signal(barrier, inc=1, device_id=peer, device_id_type=MESH)
    pl.semaphore_wait(barrier, 6)

    def rows(k):
        return pl.ds(START[k], SIZES[k])

    def pair(k, half):
        return pl.ds(2 * START[k] + half * SIZES[k], SIZES[k])

    def in_remote(k):
        return remote(x_ref.at[rows(k)], bi.at[rows(k)], in_s.at[k], in_r.at[k], swap)

    def in_local(k):
        return pltpu.make_async_copy(x_ref.at[rows(k)], bi.at[rows(k)], in_r.at[k])

    def z_in(k):
        return remote(bi.at[rows(k)], bp.at[pair(k, 0)], zi_s.at[k], zi_r.at[k], zp)

    def z_direct(k):
        return remote(x_ref.at[rows(k)], bp.at[pair(k, 0)], zi_s.at[k], zi_r.at[k], zp)

    def c_in(k):
        return remote(bp.at[pair(k, 0)], bp.at[pair(k, 1)], ci_s.at[k], ci_r.at[k], core)

    def c_back(k):
        return remote(back.at[pair(k, 1)], cr.at[rows(k)], cb_s.at[k], cb_r.at[k], core)

    def z_back(k):
        return remote(zs.at[rows(k)], zr.at[rows(k)], zb_s.at[k], zb_r.at[k], zm)

    def out_remote(k):
        return remote(os_.at[rows(k)], out_ref.at[rows(k)], o_s.at[k], o_r.at[k], swap)

    def out_local(k):
        return pltpu.make_async_copy(os_.at[rows(k)], out_ref.at[rows(k)], o_r.at[k])

    def own_remote(k):
        return remote(os_.at[rows(k)], ow.at[rows(k)], w_s.at[k], w_r.at[k], swap)

    def out_sum(k):
        return pltpu.make_async_copy(os2.at[rows(k)], out_ref.at[rows(k)], o_r.at[k])

    far = lax.rem(x + 2, 4)
    low = lax.rem(x + 3, 4)
    high = lax.rem(x + 1, 4)

    def part(shard, begin, count):
        return pl.ds(pl.multiple_of(shard * S + begin, H), count)

    def of(refs, t):
        return refs[KIND[t]].at[PLACE[t]]

    def rs1(t):
        src, dst = of(s1, t), of(r1, t)
        return (
            remote(src.at[pl.ds(0, H)], dst.at[0], x_s.at[0, t], x_r.at[0, t], xm),
            remote(src.at[pl.ds(H, H)], dst.at[1], x_s.at[1, t], x_r.at[1, t], xp),
        )

    def rs2(t):
        src, dst = of(s2, t), of(r2, t)
        return (
            remote(src.at[0], dst.at[0], x_s.at[2, t], x_r.at[2, t], xm),
            remote(src.at[1], dst.at[1], x_s.at[3, t], x_r.at[3, t], xp),
        )

    def ag1(t):
        mine = of(tt, t).at[part(x, 0, S)]
        return (
            remote(mine, mine, x_s.at[4, t], x_r.at[4, t], xm),
            remote(mine, mine, x_s.at[5, t], x_r.at[5, t], xp),
        )

    def ag2(t):
        up = of(tt, t).at[part(low, 0, H)]
        down = of(tt, t).at[part(high, H, H)]
        return (
            remote(down, down, x_s.at[6, t], x_r.at[6, t], xm),
            remote(up, up, x_s.at[7, t], x_r.at[7, t], xp),
        )

    def start(copies):
        for copy in copies:
            copy.start()

    def wait_recv(copies):
        for copy in copies:
            copy.wait_recv()

    def direct(k):
        @pl.when(last == 1)
        def _():
            z_direct(k).start()

    for k in range(K):
        @pl.when(cross)
        def _():
            in_remote(k).start()

        @pl.when(straight)
        def _():
            in_local(k).start()

        if k < 2:
            direct(k)

    def forward(k):
        @pl.when(cross)
        def _():
            in_remote(k).wait_recv()

        @pl.when(straight)
        def _():
            in_local(k).wait()

        @pl.when(last == 0)
        def _():
            z_in(k).start()

    def spread(k):
        z_in(k).wait_recv()
        c_in(k).start()

    def dot(a, b, over):
        return lax.dot_general(a, b, ((over[:1], over[1:]), ((), ())), preferred_element_type=F32)

    level = occ_ref[base + v] + occ_ref[lax.rem(base + v + 30, 32)]
    for j in range(N // 128):
        lanes = pl.ds(pl.multiple_of(c * N + j * 128, 128), 128)
        acol[j * 128 : (j + 1) * 128, :] = jnp.broadcast_to(level - vir_ref[0:1, lanes], (128, 128)).T

    def stage_a(t):
        a, b = TILES[t]
        width = 2 * SIZES[b]
        slot = t % SLOTS
        vf[slot, :, 0:width] = dot(
            bi[a * R : (a + 1) * R], bp[2 * START[b] : 2 * START[b] + width], (1, 1)
        )
        of(s1, t)[...] = vf[slot, part(far, 0, S), 0:width].astype(BF16)
        start(rs1(t))

    def stage_b(t):
        slot = t % SLOTS
        width = 2 * SIZES[TILES[t][1]]
        wait_recv(rs1(t))
        got, put = of(r1, t), of(s2, t)
        put[0, 0:H] = (vf[slot, part(low, 0, H), 0:width] + got[0].astype(F32)).astype(BF16)
        put[0, H:S] = vf[slot, part(low, H, H), 0:width].astype(BF16)
        put[1, 0:H] = vf[slot, part(high, 0, H), 0:width].astype(BF16)
        put[1, H:S] = (vf[slot, part(high, H, H), 0:width] + got[1].astype(F32)).astype(BF16)
        start(rs2(t))

    def stage_c(t):
        a, b = TILES[t]
        size = SIZES[b]
        slot = t % SLOTS
        wait_recv(rs2(t))
        got, put = of(r2, t), of(tt, t)
        level_a = acol[pl.ds(pl.multiple_of(a * R + x * S, S), S), 0:1]
        for half in (0, 1):
            cols = slice(half * size, (half + 1) * size)
            total = vf[slot, part(x, 0, S), cols] + got[0, :, cols].astype(F32) + got[1, :, cols].astype(F32)
            begin = (c + half - 2 * c * half) * N + START[b]
            gap = level_a - vir_ref[0:1, pl.ds(pl.multiple_of(begin, 128), size)]
            put[part(x, 0, S), cols] = (total / gap).astype(BF16)
        start(ag1(t))

    def stage_d(t):
        wait_recv(ag1(t))
        start(ag2(t))

    def stage_e(t):
        a, b = TILES[t]
        wait_recv(ag2(t))
        own_rows = slice(a * R, (a + 1) * R)
        pair_rows = slice(2 * START[b], 2 * START[b] + 2 * SIZES[b])
        tile = of(tt, t)[...]
        term = dot(tile, bi[own_rows], (0, 0))
        if all(other[1] != b for other in TILES[:t]):
            back[pair_rows] = term
        else:
            back[pair_rows] += term
        if COL_END[b] == t:
            c_back(b).start()
        term = dot(tile, bp[pair_rows], (1, 0))
        if all(other[0] != a for other in TILES[:t]):
            own[own_rows] = term
        else:
            own[own_rows] += term

    def stage_f(k):
        r = slice(START[k], START[k] + SIZES[k])
        c_back(k).wait_recv()
        zs[r] = (back[2 * START[k] : 2 * START[k] + SIZES[k]] + cr[r]).astype(BF16)
        z_back(k).start()

    def stage_g(k):
        r = slice(START[k], START[k] + SIZES[k])

        @pl.when(cross_last)
        def _():
            os_[r] = own[r].astype(BF16)
            own_remote(k).start()

        @pl.when(last == 0)
        def _():
            z_back(k).wait_recv()
            os_[r] = (own[r] + zr[r].astype(F32)).astype(BF16)

            @pl.when(cross)
            def _():
                out_remote(k).start()

            @pl.when(straight)
            def _():
                out_local(k).start()

    def stage_h(k):
        r = slice(START[k], START[k] + SIZES[k])

        @pl.when(cross_last)
        def _():
            own_remote(k).wait_recv()
            z_back(k).wait_recv()
            os2[r] = (ow[r].astype(F32) + zr[r].astype(F32)).astype(BF16)
            out_sum(k).start()

        @pl.when(straight_last)
        def _():
            z_back(k).wait_recv()
            os_[r] = (own[r] + zr[r].astype(F32)).astype(BF16)
            out_local(k).start()

    done_f, done_g, done_h = set(), {}, set()
    for it in range(NT + OFF["E"]):
        for name, stage in (("D", stage_d), ("C", stage_c), ("B", stage_b)):
            t = it - OFF[name]
            if 0 <= t < NT:
                stage(t)
        if it < NT:
            a, b = TILES[it]
            for k in DIRECT.get(it, []):
                direct(k)
            for k in FORWARD.get(it, []):
                forward(k)
            for k in SPREAD.get(it, []):
                spread(k)
            if all(other[1] != b for other in TILES[:it]):
                c_in(b).wait_recv()
            stage_a(it)
        t = it - OFF["E"]
        for k in range(K):
            if k not in done_f and t > COL_END[k]:
                stage_f(k)
                done_f.add(k)
        if 0 <= t < NT:
            stage_e(t)
        for k in range(K):
            if k not in done_g and COL_END[k] + 3 <= t and ROW_END[START[k] // R] <= t:
                stage_g(k)
                done_g[k] = t
    for k in range(K):
        if k not in done_f:
            stage_f(k)
    for k in range(K):
        if k not in done_g:
            stage_g(k)
    for k in range(K):
        if k not in done_h:
            stage_h(k)

    for t in range(NT):
        for group in (rs1(t), rs2(t), ag1(t), ag2(t)):
            for copy in group:
                copy.wait_send()
    for k in range(K):
        @pl.when(last == 0)
        def _():
            z_in(k).wait_send()

        @pl.when(last == 1)
        def _():
            z_direct(k).wait_send()

        c_in(k).wait_send()
        c_back(k).wait_send()
        z_back(k).wait_send()

        @pl.when(cross)
        def _():
            in_remote(k).wait_send()

        @pl.when(cross_inner)
        def _():
            out_remote(k).wait()

        @pl.when(cross_last)
        def _():
            own_remote(k).wait_send()
            out_sum(k).wait()

        @pl.when(straight)
        def _():
            out_local(k).wait()


def on_device(integrals, occ_energy, vir_energy):
    dma = pltpu.SemaphoreType.DMA
    vmem = pltpu.VMEM

    def tiles(*lead):
        return [vmem((COUNT[kind], *lead, 2 * (WIDE >> kind)), BF16) for kind in (0, 1)]

    out = pl.pallas_call(
        kernel,
        out_shape=jax.ShapeDtypeStruct((N, N), BF16),
        in_specs=[
            pl.BlockSpec(memory_space=pl.ANY),
            pl.BlockSpec(memory_space=pltpu.SMEM),
            pl.BlockSpec(memory_space=pltpu.VMEM),
        ],
        out_specs=pl.BlockSpec(memory_space=pl.ANY),
        scratch_shapes=[
            vmem((N, N), BF16),
            vmem((2 * N, N), BF16),
            vmem((N, 128), F32),
            vmem((SLOTS, R, 2 * WIDE), F32),
            *tiles(S),
            *tiles(2, S),
            *tiles(2, H),
            *tiles(2, S),
            *tiles(R),
            vmem((N, N), F32),
            vmem((2 * N, N), F32),
            vmem((N, N), F32),
            vmem((N, N), BF16),
            vmem((N, N), BF16),
            vmem((N, N), BF16),
            vmem((N, N), BF16),
            vmem((N, N), BF16),
            *[dma((K,))] * 6,
            dma((8, NT)), dma((8, NT)),
            *[dma((K,))] * 8,
        ],
        compiler_params=pltpu.CompilerParams(
            collective_id=0, has_side_effects=True, vmem_limit_bytes=58 * 2**20
        ),
        cost_estimate=pl.CostEstimate(flops=13 * 10**9, bytes_accessed=4 * 2**20, transcendentals=0),
        name="pair_lagrangian",
    )(integrals.reshape(N, N), occ_energy, vir_energy.reshape(1, 2 * N))
    return out.reshape(1, N, N)


def solution(mesh):
    placed = (P("occ", "vir", "aux"), P(), P())
    return jax.shard_map(
        on_device, mesh=mesh, in_specs=placed, out_specs=P("occ", "vir", "aux"), check_vma=False
    )
```

```python
import functools

import jax
import jax.numpy as jnp
from jax import lax
from jax.experimental import pallas as pl
from jax.experimental.pallas import tpu as pltpu
from jax.sharding import PartitionSpec as P

MESH = pl.DeviceIdType.MESH
BF16 = jnp.bfloat16
F32 = jnp.float32

N = 1024
R = 256
S = R // 4
H = S // 2
SLOTS = 6

SIZES = [128, 128, 256, 256, 128, 128]
K = len(SIZES)
START = [sum(SIZES[:k]) for k in range(K)]
ROWS = N // R
NEEDS = [[k for k in range(K) if START[k] // R == a] for a in range(ROWS)]

TILES = [(0, 0), (1, 0), (0, 1), (1, 1), (2, 0), (2, 1), (0, 2), (1, 2), (3, 0), (3, 1), (2, 2), (3, 2)]
TILES += [(a, 3) for a in range(ROWS)] + [(0, 4), (0, 5), (1, 4), (1, 5), (2, 4), (3, 4), (2, 5), (3, 5)]
NT = len(TILES)
WIDE = max(SIZES)
KIND = [0 if SIZES[b] == WIDE else 1 for a, b in TILES]
PLACE = [KIND[:t].count(KIND[t]) for t in range(NT)]
COUNT = [KIND.count(0), KIND.count(1)]
ROW_END = [max(t for t, tile in enumerate(TILES) if tile[0] == a) for a in range(ROWS)]
COL_END = [max(t for t, tile in enumerate(TILES) if tile[1] == b) for b in range(K)]

OFF = {"A": 0, "B": 2, "C": 5, "D": 7, "E": 8}
FORWARD = {0: [0, 1], 1: [2], 3: [3], 5: [4], 6: [5]}
DIRECT = {3: [2], 6: [3], 8: [4], 10: [5]}
SPREAD = {0: [0], 2: [1], 5: [2], 9: [3], 12: [4], 14: [5]}


def kernel(
    x_ref, occ_ref, vir_ref, out_ref,
    bi, bp, acol, vf, s1w, s1n, s2w, s2n, r1w, r1n, r2w, r2n, ttw, ttn, own, back, cr, zs, zr, os_, ow, os2,
    in_s, in_r, zi_s, zi_r, ci_s, ci_r, x_s, x_r, cb_s, cb_r, zb_s, zb_r, o_s, o_r, w_s, w_r,
):
    o, x, v = lax.axis_index("occ"), lax.axis_index("aux"), lax.axis_index("vir")
    c = lax.rem(o, 2)
    base = o - c
    z = lax.rem(o, 16) // 2
    last = z // 7
    first = 1 - (z + 7) // 8
    cross = c + v == 1
    straight = c + v != 1
    straight_last = last - lax.rem(c + v, 2) == 1
    cross_last = lax.rem(c + v, 2) + last == 2
    cross_inner = lax.rem(c + v, 2) - last == 1
    xp = (o, lax.rem(x + 1, 4), v)
    xm = (o, lax.rem(x + 3, 4), v)
    zp = (lax.rem(base + 2, 32) + c + last * (v - c), x, v + last * (c - v))
    zm = (lax.rem(base + 30, 32) + c + first * (v - c), x, v + first * (c - v))
    core = (base + 1 - c, x, v)
    swap = (base + 1 - c, x, 1 - v)
    s1, s2, r1, r2, tt = (s1w, s1n), (s2w, s2n), (r1w, r1n), (r2w, r2n), (ttw, ttn)

    def remote(src, dst, ssem, rsem, to):
        return pltpu.make_async_remote_copy(
            src_ref=src, dst_ref=dst, send_sem=ssem, recv_sem=rsem, device_id=to, device_id_type=MESH
        )

    barrier = pltpu.get_barrier_semaphore()
    for peer in (xp, xm, zp, zm, core, swap):
        pl.semaphore_signal(barrier, inc=1, device_id=peer, device_id_type=MESH)
    pl.semaphore_wait(barrier, 6)

    def rows(k):
        return pl.ds(START[k], SIZES[k])

    def pair(k, half):
        return pl.ds(2 * START[k] + half * SIZES[k], SIZES[k])

    def in_remote(k):
        return remote(x_ref.at[rows(k)], bi.at[rows(k)], in_s.at[k], in_r.at[k], swap)

    def in_local(k):
        return pltpu.make_async_copy(x_ref.at[rows(k)], bi.at[rows(k)], in_r.at[k])

    def z_in(k):
        return remote(bi.at[rows(k)], bp.at[pair(k, 0)], zi_s.at[k], zi_r.at[k], zp)

    def z_direct(k):
        return remote(x_ref.at[rows(k)], bp.at[pair(k, 0)], zi_s.at[k], zi_r.at[k], zp)

    def c_in(k):
        return remote(bp.at[pair(k, 0)], bp.at[pair(k, 1)], ci_s.at[k], ci_r.at[k], core)

    def c_back(k):
        return remote(back.at[pair(k, 1)], cr.at[rows(k)], cb_s.at[k], cb_r.at[k], core)

    def z_back(k):
        return remote(zs.at[rows(k)], zr.at[rows(k)], zb_s.at[k], zb_r.at[k], zm)

    def out_remote(k):
        return remote(os_.at[rows(k)], out_ref.at[rows(k)], o_s.at[k], o_r.at[k], swap)

    def out_local(k):
        return pltpu.make_async_copy(os_.at[rows(k)], out_ref.at[rows(k)], o_r.at[k])

    def own_remote(k):
        return remote(os_.at[rows(k)], ow.at[rows(k)], w_s.at[k], w_r.at[k], swap)

    def out_sum(k):
        return pltpu.make_async_copy(os2.at[rows(k)], out_ref.at[rows(k)], o_r.at[k])

    far = lax.rem(x + 2, 4)
    low = lax.rem(x + 3, 4)
    high = lax.rem(x + 1, 4)

    def part(shard, begin, count):
        return pl.ds(pl.multiple_of(shard * S + begin, H), count)

    def of(refs, t):
        return refs[KIND[t]].at[PLACE[t]]

    def rs1(t):
        src, dst = of(s1, t), of(r1, t)
        return (
            remote(src.at[pl.ds(0, H)], dst.at[0], x_s.at[0, t], x_r.at[0, t], xm),
            remote(src.at[pl.ds(H, H)], dst.at[1], x_s.at[1, t], x_r.at[1, t], xp),
        )

    def rs2(t):
        src, dst = of(s2, t), of(r2, t)
        return (
            remote(src.at[0], dst.at[0], x_s.at[2, t], x_r.at[2, t], xm),
            remote(src.at[1], dst.at[1], x_s.at[3, t], x_r.at[3, t], xp),
        )

    def ag1(t):
        mine = of(tt, t).at[part(x, 0, S)]
        return (
            remote(mine, mine, x_s.at[4, t], x_r.at[4, t], xm),
            remote(mine, mine, x_s.at[5, t], x_r.at[5, t], xp),
        )

    def ag2(t):
        up = of(tt, t).at[part(low, 0, H)]
        down = of(tt, t).at[part(high, H, H)]
        return (
            remote(down, down, x_s.at[6, t], x_r.at[6, t], xm),
            remote(up, up, x_s.at[7, t], x_r.at[7, t], xp),
        )

    def start(copies):
        for copy in copies:
            copy.start()

    def wait_recv(copies):
        for copy in copies:
            copy.wait_recv()

    def direct(k):
        @pl.when(last == 1)
        def _():
            z_direct(k).start()

    for k in range(K):
        @pl.when(cross)
        def _():
            in_remote(k).start()

        @pl.when(straight)
        def _():
            in_local(k).start()

        if k < 2:
            direct(k)

    def forward(k):
        @pl.when(cross)
        def _():
            in_remote(k).wait_recv()

        @pl.when(straight)
        def _():
            in_local(k).wait()

        @pl.when(last == 0)
        def _():
            z_in(k).start()

    def spread(k):
        z_in(k).wait_recv()
        c_in(k).start()

    def dot(a, b, over):
        return lax.dot_general(a, b, ((over[:1], over[1:]), ((), ())), preferred_element_type=F32)

    level = occ_ref[base + v] + occ_ref[lax.rem(base + v + 30, 32)]
    for j in range(N // 128):
        lanes = pl.ds(pl.multiple_of(c * N + j * 128, 128), 128)
        acol[j * 128 : (j + 1) * 128, :] = jnp.broadcast_to(level - vir_ref[0:1, lanes], (128, 128)).T

    def stage_a(t):
        a, b = TILES[t]
        width = 2 * SIZES[b]
        slot = t % SLOTS
        vf[slot, :, 0:width] = dot(
            bi[a * R : (a + 1) * R], bp[2 * START[b] : 2 * START[b] + width], (1, 1)
        )
        of(s1, t)[...] = vf[slot, part(far, 0, S), 0:width].astype(BF16)
        start(rs1(t))

    def stage_b(t):
        slot = t % SLOTS
        width = 2 * SIZES[TILES[t][1]]
        wait_recv(rs1(t))
        got, put = of(r1, t), of(s2, t)
        put[0, 0:H] = (vf[slot, part(low, 0, H), 0:width] + got[0].astype(F32)).astype(BF16)
        put[0, H:S] = vf[slot, part(low, H, H), 0:width].astype(BF16)
        put[1, 0:H] = vf[slot, part(high, 0, H), 0:width].astype(BF16)
        put[1, H:S] = (vf[slot, part(high, H, H), 0:width] + got[1].astype(F32)).astype(BF16)
        start(rs2(t))

    def stage_c(t):
        a, b = TILES[t]
        size = SIZES[b]
        slot = t % SLOTS
        wait_recv(rs2(t))
        got, put = of(r2, t), of(tt, t)
        level_a = acol[pl.ds(pl.multiple_of(a * R + x * S, S), S), 0:1]
        for half in (0, 1):
            cols = slice(half * size, (half + 1) * size)
            total = vf[slot, part(x, 0, S), cols] + got[0, :, cols].astype(F32) + got[1, :, cols].astype(F32)
            begin = (c + half - 2 * c * half) * N + START[b]
            gap = level_a - vir_ref[0:1, pl.ds(pl.multiple_of(begin, 128), size)]
            put[part(x, 0, S), cols] = (total / gap).astype(BF16)
        start(ag1(t))

    def stage_d(t):
        wait_recv(ag1(t))
        start(ag2(t))

    def stage_e(t):
        a, b = TILES[t]
        wait_recv(ag2(t))
        own_rows = slice(a * R, (a + 1) * R)
        pair_rows = slice(2 * START[b], 2 * START[b] + 2 * SIZES[b])
        tile = of(tt, t)[...]
        term = dot(tile, bi[own_rows], (0, 0))
        if all(other[1] != b for other in TILES[:t]):
            back[pair_rows] = term
        else:
            back[pair_rows] += term
        if COL_END[b] == t:
            c_back(b).start()
        term = dot(tile, bp[pair_rows], (1, 0))
        if all(other[0] != a for other in TILES[:t]):
            own[own_rows] = term
        else:
            own[own_rows] += term

    def stage_f(k):
        r = slice(START[k], START[k] + SIZES[k])
        c_back(k).wait_recv()
        zs[r] = (back[2 * START[k] : 2 * START[k] + SIZES[k]] + cr[r]).astype(BF16)
        z_back(k).start()

    def stage_g(k):
        r = slice(START[k], START[k] + SIZES[k])

        @pl.when(cross_last)
        def _():
            os_[r] = own[r].astype(BF16)
            own_remote(k).start()

        @pl.when(last == 0)
        def _():
            z_back(k).wait_recv()
            os_[r] = (own[r] + zr[r].astype(F32)).astype(BF16)

            @pl.when(cross)
            def _():
                out_remote(k).start()

            @pl.when(straight)
            def _():
                out_local(k).start()

    def stage_h(k):
        r = slice(START[k], START[k] + SIZES[k])

        @pl.when(cross_last)
        def _():
            own_remote(k).wait_recv()
            z_back(k).wait_recv()
            os2[r] = (ow[r].astype(F32) + zr[r].astype(F32)).astype(BF16)
            out_sum(k).start()

        @pl.when(straight_last)
        def _():
            z_back(k).wait_recv()
            os_[r] = (own[r] + zr[r].astype(F32)).astype(BF16)
            out_local(k).start()

    done_f, done_g, done_h = set(), {}, set()
    for it in range(NT + OFF["E"]):
        for name, stage in (("D", stage_d), ("C", stage_c), ("B", stage_b)):
            t = it - OFF[name]
            if 0 <= t < NT:
                stage(t)
        if it < NT:
            a, b = TILES[it]
            for k in DIRECT.get(it, []):
                direct(k)
            for k in FORWARD.get(it, []):
                forward(k)
            for k in SPREAD.get(it, []):
                spread(k)
            if all(other[1] != b for other in TILES[:it]):
                c_in(b).wait_recv()
            stage_a(it)
        t = it - OFF["E"]
        for k in range(K):
            if k not in done_f and t > COL_END[k]:
                stage_f(k)
                done_f.add(k)
        if 0 <= t < NT:
            stage_e(t)
        for k in range(K):
            if k not in done_g and COL_END[k] + 3 <= t and ROW_END[START[k] // R] <= t:
                stage_g(k)
                done_g[k] = t
    for k in range(K):
        if k not in done_f:
            stage_f(k)
    for k in range(K):
        if k not in done_g:
            stage_g(k)
    for k in range(K):
        if k not in done_h:
            stage_h(k)

    for t in range(NT):
        for group in (rs1(t), rs2(t), ag1(t), ag2(t)):
            for copy in group:
                copy.wait_send()
    for k in range(K):
        @pl.when(last == 0)
        def _():
            z_in(k).wait_send()

        @pl.when(last == 1)
        def _():
            z_direct(k).wait_send()

        c_in(k).wait_send()
        c_back(k).wait_send()
        z_back(k).wait_send()

        @pl.when(cross)
        def _():
            in_remote(k).wait_send()

        @pl.when(cross_inner)
        def _():
            out_remote(k).wait()

        @pl.when(cross_last)
        def _():
            own_remote(k).wait_send()
            out_sum(k).wait()

        @pl.when(straight)
        def _():
            out_local(k).wait()


def on_device(integrals, occ_energy, vir_energy):
    dma = pltpu.SemaphoreType.DMA
    vmem = pltpu.VMEM

    def tiles(*lead):
        return [vmem((COUNT[kind], *lead, 2 * (WIDE >> kind)), BF16) for kind in (0, 1)]

    out = pl.pallas_call(
        kernel,
        out_shape=jax.ShapeDtypeStruct((N, N), BF16),
        in_specs=[
            pl.BlockSpec(memory_space=pl.ANY),
            pl.BlockSpec(memory_space=pltpu.SMEM),
            pl.BlockSpec(memory_space=pltpu.VMEM),
        ],
        out_specs=pl.BlockSpec(memory_space=pl.ANY),
        scratch_shapes=[
            vmem((N, N), BF16),
            vmem((2 * N, N), BF16),
            vmem((N, 128), F32),
            vmem((SLOTS, R, 2 * WIDE), F32),
            *tiles(S),
            *tiles(2, S),
            *tiles(2, H),
            *tiles(2, S),
            *tiles(R),
            vmem((N, N), F32),
            vmem((2 * N, N), F32),
            vmem((N, N), F32),
            vmem((N, N), BF16),
            vmem((N, N), BF16),
            vmem((N, N), BF16),
            vmem((N, N), BF16),
            vmem((N, N), BF16),
            *[dma((K,))] * 6,
            dma((8, NT)), dma((8, NT)),
            *[dma((K,))] * 8,
        ],
        compiler_params=pltpu.CompilerParams(
            collective_id=0, has_side_effects=True, vmem_limit_bytes=58 * 2**20
        ),
        cost_estimate=pl.CostEstimate(flops=13 * 10**9, bytes_accessed=4 * 2**20, transcendentals=0),
        name="pair_lagrangian",
    )(integrals.reshape(N, N), occ_energy, vir_energy.reshape(1, 2 * N))
    return out.reshape(1, N, N)


def solution(mesh):
    placed = (P("occ", "vir", "aux"), P(), P())
    return jax.shard_map(
        on_device, mesh=mesh, in_specs=placed, out_specs=P("occ", "vir", "aux"), check_vma=False
    )
```
